32 devices in a mesh: parts: 2 (over y), space: 8 (over z, x), tm: 2 (over core).
Axes of the slice: x: 2, y: 2, z: 4, core: 2. Of those that a mesh axis runs over, the one named last changes fastest.
Arguments:
- eigvecs: bfloat16 [4, 2, 256, 3, 1728], P(('parts', 'tm'), None, None, None, 'space'), parts along dimension 0, may hold values from -1.25 to 1.25
- links: bfloat16 [4, 3, 3, 3, 2, 1728], P(('parts', 'tm'), None, None, None, None, 'space'), parts along dimension 0, may hold values from -2.5 to 2.5
- dirs: int32 [3], replicated, may hold values from 0 to 2, each once
- peram: bfloat16 [4, 2, 1024, 1024], P(('parts', 'tm'), None, 'space'), parts along dimension 0, may hold values from -0.25 to 0.25
Outputs:
- meson_blocks: bfloat16 [4, 3, 2, 1024, 1024], P(('parts', 'tm'), None, None, 'space'), parts along dimension 0
The draws below stay inside these ranges and needn't reach their ends.
There are 2 independent parts, one for each index of `parts`. The reference program is written for one: setup_inputs(seed, part) draws one part's arguments, and reference() takes and returns one part's arrays. A program takes and returns all parts, laid end to end along the dimension named above; an argument that names none is the same for every part. Nothing has to cross between parts.
All inputs are finite; a program needn't handle non-finite values.
Results may differ from the reference program's by a relative error of at most 0.0061.
Values may be sent and summed in bfloat16 or wider, within the bound.
A program may use at most 64 MiB of HBM per device.

```python
import jax
import jax.numpy as jnp
from jax import lax

K = 256
SPIN = 4
NDIR = 3
TS = 1
LX = 9
LZ = 24
LY = 8
SITES = 1728
NT = 2


def level_of(rng, shape, pieces, low, high):
    factor_of = 1.0
    for dim, shards_of in pieces:
        draws = jax.random.uniform(jax.random.fold_in(jax.random.fold_in(rng, 6), dim), (shards_of,), jnp.float32, low / len(pieces), high / len(pieces))
        factor_of = factor_of * jnp.repeat(jnp.exp(draws), shape[dim] // shards_of).reshape((-1,) + (1,) * (len(shape) - 1 - dim))
    return factor_of


def centred(own_key, dims, deviation, limit, cuts=(), kind=jnp.bfloat16):
    loudness = level_of(own_key, dims, cuts, -0.22, 0.18) if cuts else 1.0
    values = jax.random.normal(own_key, dims, jnp.float32) * deviation * loudness
    return jnp.minimum(jnp.maximum(values, -limit), limit).astype(kind)


def setup_inputs(seed: int = 0, part: int = 0) -> dict:
    key_of = jax.random.split(jax.random.key(seed), 5)
    part_keys = jax.random.split(jax.random.fold_in(key_of[4], part), 5)
    return {
        "eigvecs": centred(part_keys[0], (NT, 2, K, 3, SITES), (0.85 * (6 * SITES) ** -0.25), 1.25, ((0, 2), (4, 8))),
        "links": centred(part_keys[1], (NT, 3, 3, 3, 2, SITES), 0.4, 2.5, ((0, 2), (5, 8))),
        "dirs": jax.random.permutation(key_of[2], 3).astype(jnp.int32),
        "peram": centred(part_keys[3], (NT, 2, K * SPIN, K * SPIN), (2 * K) ** -0.5, 0.25, ((0, 2), (2, 8))),
    }


def to_lattice(values):
    return values.reshape(values.shape[:-1] + (LY, LX, LZ))


def link_apply(link_mat, values_in, adjoint):
    real_rows = []
    imag_rows = []
    for out_row in range(3):
        real_sum = jnp.zeros(values_in.shape[1:2] + values_in.shape[3:], jnp.float32)
        imag_sum = jnp.zeros(values_in.shape[1:2] + values_in.shape[3:], jnp.float32)
        for in_col in range(3):
            if adjoint:
                link_entry = link_mat[in_col, out_row]
                conj_sign = -1.0
            else:
                link_entry = link_mat[out_row, in_col]
                conj_sign = 1.0
            link_real = link_entry[0].astype(jnp.float32)[None]
            link_imag = (conj_sign * link_entry[1].astype(jnp.float32))[None]
            vec_real = values_in[0, :, in_col].astype(jnp.float32)
            vec_imag = values_in[1, :, in_col].astype(jnp.float32)
            real_sum = real_sum + link_real * vec_real - link_imag * vec_imag
            imag_sum = imag_sum + link_real * vec_imag + link_imag * vec_real
        real_rows.append(real_sum)
        imag_rows.append(imag_sum)
    return jnp.stack([jnp.stack(real_rows, axis=1), jnp.stack(imag_rows, axis=1)])


def neighbour(values_in, direction, step_size):
    lattice_axis = (-2, -3, -1)[direction]
    return jnp.roll(values_in, -step_size, axis=lattice_axis)


def contract(left, right):
    return lax.dot_general(left, right, (((1,), (1,)), ((), ())), preferred_element_type=jnp.float32)


def elemental(eigen_field, derivative):
    vectors = eigen_field.shape[1]
    vec_real = eigen_field[0].reshape(vectors, -1)
    vec_imag = eigen_field[1].reshape(vectors, -1)
    der_real = derivative[0].reshape(vectors, -1)
    der_imag = derivative[1].reshape(vectors, -1)
    return jnp.stack([contract(vec_real, der_real) + contract(vec_imag, der_imag),
                      contract(vec_real, der_imag) - contract(vec_imag, der_real)])


def reference(eigvecs, links, dirs, peram):
    choose = dirs[:, None] == jnp.arange(3, dtype=jnp.int32)[None, :]
    columns = peram.shape[2]
    groups = NT // TS
    results = []
    for time_slice in range(NT):
        eigen_field = to_lattice(eigvecs[time_slice])
        links_now = to_lattice(links[time_slice])
        elementals = []
        for direction in range(3):
            back_term = link_apply(links_now[direction], eigen_field, True).astype(jnp.bfloat16)
            ahead_term = link_apply(links_now[direction], neighbour(eigen_field, direction, 1), False)
            derivative = (ahead_term - neighbour(back_term, direction, -1).astype(jnp.float32)).astype(jnp.bfloat16)
            elementals.append(elemental(eigen_field, derivative))
        elementals = jnp.stack(elementals)
        picked = jnp.sum(jnp.where(choose[:, :, None, None, None], elementals[None], 0.0), axis=1)
        elem_low = picked.astype(jnp.bfloat16)
        partner_slice = ((time_slice // TS + 1) % groups) * TS + time_slice % TS
        peram_block = peram[partner_slice]
        elem_real = elem_low[:, 0].astype(jnp.float32)
        elem_imag = elem_low[:, 1].astype(jnp.float32)
        peram_real = peram_block[0].astype(jnp.float32).reshape(columns, K, SPIN)
        peram_imag = peram_block[1].astype(jnp.float32).reshape(columns, K, SPIN)
        highest = lax.Precision.HIGHEST
        out_real = (jnp.einsum('jkl,cls->jcks', elem_real, peram_real, precision=highest)
                    - jnp.einsum('jkl,cls->jcks', elem_imag, peram_imag, precision=highest))
        out_imag = (jnp.einsum('jkl,cls->jcks', elem_real, peram_imag, precision=highest)
                    + jnp.einsum('jkl,cls->jcks', elem_imag, peram_real, precision=highest))
        stacked = jnp.stack([out_real, out_imag], axis=1)
        results.append(stacked.reshape(NDIR, 2, columns, K * SPIN).astype(jnp.bfloat16))
    return jnp.stack(results)
```

```python
import functools

import jax
import jax.numpy as jnp
import numpy as np
from jax import lax
from jax.experimental import pallas as pl
from jax.experimental.pallas import tpu as pltpu
from jax.sharding import PartitionSpec as P

K = 256
SPIN = 4
LX = 9
LZ = 24
MESH = pl.DeviceIdType.MESH


def from_behind(block, axis, distance):
    devices = range(lax.axis_size(axis))
    route = [((i - distance) % len(devices), i) for i in devices]
    return lax.ppermute(block, axis, route)


def link_apply(link_mat, values_in, adjoint):
    real_rows = []
    imag_rows = []
    for out_row in range(3):
        real_sum = jnp.zeros(values_in.shape[1:2] + values_in.shape[3:], jnp.float32)
        imag_sum = jnp.zeros(values_in.shape[1:2] + values_in.shape[3:], jnp.float32)
        for in_col in range(3):
            if adjoint:
                link_entry = link_mat[in_col, out_row]
                conj_sign = -1.0
            else:
                link_entry = link_mat[out_row, in_col]
                conj_sign = 1.0
            link_real = link_entry[0].astype(jnp.float32)[None]
            link_imag = (conj_sign * link_entry[1].astype(jnp.float32))[None]
            vec_real = values_in[0, :, in_col].astype(jnp.float32)
            vec_imag = values_in[1, :, in_col].astype(jnp.float32)
            real_sum = real_sum + link_real * vec_real - link_imag * vec_imag
            imag_sum = imag_sum + link_real * vec_imag + link_imag * vec_real
        real_rows.append(real_sum)
        imag_rows.append(imag_sum)
    return jnp.stack([jnp.stack(real_rows, axis=1), jnp.stack(imag_rows, axis=1)])


def contract(left, right):
    return lax.dot_general(
        left, right, (((1,), (1,)), ((), ())), preferred_element_type=jnp.float32
    )


def elemental(eigen_field, derivative):
    vectors = eigen_field.shape[1]
    vec_real = eigen_field[0].reshape(vectors, -1)
    vec_imag = eigen_field[1].reshape(vectors, -1)
    der_real = derivative[0].reshape(vectors, -1)
    der_imag = derivative[1].reshape(vectors, -1)
    return jnp.stack(
        [
            contract(vec_real, der_real) + contract(vec_imag, der_imag),
            contract(vec_real, der_imag) - contract(vec_imag, der_real),
        ]
    )


def lattice(values):
    return values.reshape(values.shape[:-1] + (values.shape[-1] // (LX * LZ), LX, LZ))


def general(eigvecs, links, dirs, peram):
    eig_lat = lattice(eigvecs)
    link_lat = lattice(links)
    slab_rows = eig_lat.shape[4]
    back_y = jnp.stack([link_apply(link_lat[0, 1], eig_lat[0], True).astype(jnp.bfloat16)])
    y_ahead = from_behind(eig_lat[:, :, :, :, 0], "space", -1)
    y_behind = from_behind(back_y[:, :, :, :, slab_rows - 1], "space", 1)
    choose = dirs[:, None] == jnp.arange(3, dtype=jnp.int32)[None, :]
    position = 0
    eigen_field = eig_lat[position]
    link_set = link_lat[position]
    elementals = []
    for direction in range(3):
        if direction == 0:
            ahead_field = jnp.roll(eigen_field, -1, axis=4)
            back_term = link_apply(link_set[0], eigen_field, True).astype(jnp.bfloat16)
            behind = jnp.roll(back_term, 1, axis=4)
        elif direction == 1:
            ahead_field = jnp.concatenate(
                [eigen_field[:, :, :, 1:], y_ahead[position][:, :, :, None]], axis=3
            )
            behind = jnp.concatenate(
                [y_behind[position][:, :, :, None], back_y[position][:, :, :, :-1]], axis=3
            )
        else:
            ahead_field = jnp.roll(eigen_field, -1, axis=5)
            back_term = link_apply(link_set[2], eigen_field, True).astype(jnp.bfloat16)
            behind = jnp.roll(back_term, 1, axis=5)
        derivative = (
            link_apply(link_set[direction], ahead_field, False) - behind.astype(jnp.float32)
        ).astype(jnp.bfloat16)
        elementals.append(elemental(eigen_field, derivative))
    elementals = jnp.stack(elementals)
    picked_all = [jnp.sum(jnp.where(choose[:, :, None, None, None], elementals[None], 0.0), axis=1)]
    stacked = jnp.stack(picked_all)
    elem_low = lax.psum(stacked, "space").astype(jnp.bfloat16)
    return finish(elem_low, from_behind(peram, "tm", -1))


def finish(elem_low, blocks):
    columns = blocks.shape[2]
    position = 0
    elem_real = elem_low[position, :, 0]
    elem_imag = elem_low[position, :, 1]
    peram_real = blocks[position, 0].reshape(columns, K, SPIN)
    peram_imag = blocks[position, 1].reshape(columns, K, SPIN)
    out_real = jnp.einsum(
        "jkl,cls->jcks", elem_real, peram_real, preferred_element_type=jnp.float32
    ) - jnp.einsum("jkl,cls->jcks", elem_imag, peram_imag, preferred_element_type=jnp.float32)
    out_imag = jnp.einsum(
        "jkl,cls->jcks", elem_real, peram_imag, preferred_element_type=jnp.float32
    ) + jnp.einsum("jkl,cls->jcks", elem_imag, peram_real, preferred_element_type=jnp.float32)
    combined = jnp.stack([out_real, out_imag], axis=1)
    results = [combined.reshape(combined.shape[0], 2, columns, K * SPIN).astype(jnp.bfloat16)]
    return jnp.stack(results)


def halo_plan(eigvecs):
    n = lax.axis_size("space")
    return (
        eigvecs.shape[-1] == LX * LZ
        and lax.axis_size("tm") == 2
        and n > 1
        and eigvecs.shape[0] == 1
        and K % (16 * n) == 0
    )


def mix(link_ref, direction, adjoint, lanes, source, target):
    lo, hi = lanes

    @pl.loop(0, K // 16)
    def _(step):
        rows = pl.ds(pl.multiple_of(step * 16, 16), 16)
        vec = [[source(ri, c, rows).astype(jnp.float32) for c in range(3)] for ri in range(2)]
        for out_row in range(3):
            real_sum = None
            for in_col in range(3):
                a, b = (in_col, out_row) if adjoint else (out_row, in_col)
                at = ((direction * 3 + a) * 3 + b) * 2
                link_real = link_ref[at : at + 1, lo:hi]
                link_imag = link_ref[at + 1 : at + 2, lo:hi]
                rr = link_real * vec[0][in_col]
                ii = link_imag * vec[1][in_col]
                ri = link_real * vec[1][in_col]
                ir = link_imag * vec[0][in_col]
                real = rr + ii if adjoint else rr - ii
                imag = ri - ir if adjoint else ri + ir
                real_sum = real if real_sum is None else real_sum + real
                imag_sum = imag if in_col == 0 else imag_sum + imag
            target[0, out_row, rows, :] = real_sum.astype(jnp.bfloat16)
            target[1, out_row, rows, :] = imag_sum.astype(jnp.bfloat16)


def overlap(left, right):
    real = imag = None
    for c in range(3):
        lr, li, rr, ri = left(0, c), left(1, c), right(0, c), right(1, c)
        re = contract(lr, rr) + contract(li, ri)
        im = contract(lr, ri) - contract(li, rr)
        real = re if real is None else real + re
        imag = im if imag is None else imag + im
    return real, imag


def halo_kernel(
    n, v_ref, link_ref, perm_ref, peram_ref, elem_ref, swapped_ref,
    shifted, mixed, mixed_lo, up_out, up_in, down_in, part, gathered, low, landed,
    halo_send, halo_recv, rs_send, rs_recv, ag_send, ag_recv,
):
    me = lax.axis_index("space")
    core = lax.axis_index("tm")
    chunk = K // n
    split = 128
    sites = LX * LZ

    barrier = pltpu.get_barrier_semaphore()
    for o in range(1, n):
        pl.semaphore_signal(
            barrier, inc=1, device_id={"space": lax.rem(me + o, n)}, device_id_type=MESH
        )
    pl.semaphore_signal(barrier, inc=1, device_id={"tm": 1 - core}, device_id_type=MESH)
    pl.semaphore_wait(barrier, n)

    down = pltpu.make_async_remote_copy(
        src_ref=v_ref.at[:, :, :, pl.ds(0, split)],
        dst_ref=down_in,
        send_sem=halo_send.at[0],
        recv_sem=halo_recv.at[0],
        device_id={"space": lax.rem(me + n - 1, n)},
        device_id_type=MESH,
    )
    down.start()
    mix(link_ref, 1, True, (split, sites), lambda ri, c, rows: v_ref[ri, c, rows, split:sites], up_out)
    up = pltpu.make_async_remote_copy(
        src_ref=up_out,
        dst_ref=up_in,
        send_sem=halo_send.at[1],
        recv_sem=halo_recv.at[1],
        device_id={"space": lax.rem(me + 1, n)},
        device_id_type=MESH,
    )
    up.start()
    swap = pltpu.make_async_remote_copy(
        src_ref=peram_ref,
        dst_ref=swapped_ref,
        send_sem=halo_send.at[2],
        recv_sem=halo_recv.at[2],
        device_id={"tm": 1 - core},
        device_id_type=MESH,
    )
    swap.start()

    row = lax.broadcasted_iota(jnp.int32, (K, K), 0)
    col = lax.broadcasted_iota(jnp.int32, (K, K), 1)

    def scatter(direction, real, imag):
        turned = jnp.where(row > col, -real, imag).T
        part[direction] = (jnp.where(row < col, real, imag) + turned).astype(jnp.bfloat16)
        copies = []
        for o in range(1, n):
            peer = lax.rem(me + o, n)
            copy = pltpu.make_async_remote_copy(
                src_ref=part.at[direction, pl.ds(pl.multiple_of(peer * chunk, chunk), chunk)],
                dst_ref=landed.at[direction, o],
                send_sem=rs_send.at[direction, o],
                recv_sem=rs_recv.at[direction, o],
                device_id={"space": peer},
                device_id_type=MESH,
            )
            copy.start()
            copies.append(copy)
        return copies

    def gather(direction, copies):
        mine = pl.ds(pl.multiple_of(me * chunk, chunk), chunk)
        total = part[direction, mine].astype(jnp.float32)
        for o in range(1, n):
            copies[o - 1].wait_recv()
            total = total + landed[direction, o].astype(jnp.float32)
        low[direction] = total.astype(jnp.bfloat16)
        gathered[direction, mine] = low[direction]
        sends = []
        for o in range(1, n):
            copy = pltpu.make_async_remote_copy(
                src_ref=low.at[direction],
                dst_ref=gathered.at[direction, mine],
                send_sem=ag_send.at[direction, o],
                recv_sem=ag_recv.at[direction, o],
                device_id={"space": lax.rem(me + o, n)},
                device_id_type=MESH,
            )
            copy.start()
            sends.append(copy)
        return sends

    def unpack(direction, sends):
        for copy in sends:
            copy.wait_recv()
        whole = gathered[direction].astype(jnp.float32)
        flipped = whole.T
        elem_ref[direction, 0] = jnp.where(
            row < col, whole, jnp.where(row > col, -flipped, 0.0)
        ).astype(jnp.bfloat16)
        elem_ref[direction, 1] = jnp.where(row < col, flipped, whole).astype(jnp.bfloat16)

    own = lambda ri, c: v_ref[ri, c]
    scattered = {}
    for direction, which in ((0, 0), (2, 1)):
        for ri in range(2):
            for c in range(3):
                shifted[ri, c] = jnp.dot(
                    v_ref[ri, c], perm_ref[which], preferred_element_type=jnp.float32
                ).astype(jnp.bfloat16)
        mix(link_ref, direction, False, (0, sites), lambda ri, c, rows: shifted[ri, c, rows, :], mixed)
        scattered[direction] = scatter(direction, *overlap(own, lambda ri, c: mixed[ri, c]))

    down.wait_recv()
    mix(link_ref, 1, False, (0, split), lambda ri, c, rows: down_in[ri, c, rows, :], mixed_lo)
    real, imag = overlap(lambda ri, c: v_ref[ri, c, :, 0:split], lambda ri, c: mixed_lo[ri, c])
    up.wait_recv()
    real_up, imag_up = overlap(lambda ri, c: up_in[ri, c], lambda ri, c: v_ref[ri, c, :, split:sites])
    scattered[1] = scatter(1, real + real_up, imag + imag_up)

    sent = {direction: gather(direction, scattered[direction]) for direction in (0, 2, 1)}
    for direction in (0, 2, 1):
        unpack(direction, sent[direction])
    swap.wait()
    down.wait_send()
    up.wait_send()
    for direction in range(3):
        for copy in scattered[direction] + sent[direction]:
            copy.wait_send()


def shift_tables():
    site = np.arange(LX * LZ)
    x, z = site // LZ, site % LZ
    tables = []
    for source in (((x + 1) % LX) * LZ + z, x * LZ + (z + 1) % LZ):
        tables.append(site[:, None] == source[None, :])
    return jnp.asarray(np.stack(tables), jnp.bfloat16)


def exchange(eigvecs, links, peram):
    n = lax.axis_size("space")
    sites = LX * LZ
    bf, chunk = jnp.bfloat16, K // n
    vmem = pl.BlockSpec(memory_space=pltpu.VMEM)
    hbm = pl.BlockSpec(memory_space=pl.ANY)
    return pl.pallas_call(
        functools.partial(halo_kernel, n),
        out_shape=(
            jax.ShapeDtypeStruct((3, 2, K, K), bf),
            jax.ShapeDtypeStruct(peram.shape[1:], bf),
        ),
        in_specs=[vmem, vmem, vmem, hbm],
        out_specs=(vmem, hbm),
        scratch_shapes=[
            pltpu.VMEM((2, 3, K, sites), bf),
            pltpu.VMEM((2, 3, K, sites), bf),
            pltpu.VMEM((2, 3, K, 128), bf),
            pltpu.VMEM((2, 3, K, sites - 128), bf),
            pltpu.VMEM((2, 3, K, sites - 128), bf),
            pltpu.VMEM((2, 3, K, 128), bf),
            pltpu.VMEM((3, K, K), bf),
            pltpu.VMEM((3, K, K), bf),
            pltpu.VMEM((3, chunk, K), bf),
            pltpu.VMEM((3, n, chunk, K), bf),
            pltpu.SemaphoreType.DMA((3,)),
            pltpu.SemaphoreType.DMA((3,)),
            pltpu.SemaphoreType.DMA((3, n)),
            pltpu.SemaphoreType.DMA((3, n)),
            pltpu.SemaphoreType.DMA((3, n)),
            pltpu.SemaphoreType.DMA((3, n)),
        ],
        compiler_params=pltpu.CompilerParams(
            collective_id=0, has_side_effects=True, vmem_limit_bytes=40 * 2**20
        ),
    )(
        jnp.transpose(eigvecs[0], (0, 2, 1, 3)),
        links[0].reshape(54, sites).astype(jnp.float32),
        shift_tables(),
        peram[0],
    )


def on_device(eigvecs, links, dirs, peram):
    if halo_plan(eigvecs):
        elem, swapped = exchange(eigvecs, links, peram)
        picked = [
            jnp.where(dirs[j] == 0, elem[0], jnp.where(dirs[j] == 1, elem[1], elem[2]))
            for j in range(3)
        ]
        return finish(jnp.stack(picked)[None], swapped[None])
    return general(eigvecs, links, dirs, peram)


def solution(mesh):
    placed = (
        P(("parts", "tm"), None, None, None, "space"),
        P(("parts", "tm"), None, None, None, None, "space"),
        P(),
        P(("parts", "tm"), None, "space", None),
    )
    return jax.shard_map(
        on_device,
        mesh=mesh,
        in_specs=placed,
        out_specs=P(("parts", "tm"), None, None, "space", None),
        check_vma=False,
    )
```

```python
import functools

import jax
import jax.numpy as jnp
import numpy as np
from jax import lax
from jax.experimental import pallas as pl
from jax.experimental.pallas import tpu as pltpu
from jax.sharding import PartitionSpec as P

K = 256
SPIN = 4
LX = 9
LZ = 24
MESH = pl.DeviceIdType.MESH


def from_behind(block, axis, distance):
    devices = range(lax.axis_size(axis))
    route = [((i - distance) % len(devices), i) for i in devices]
    return lax.ppermute(block, axis, route)


def link_apply(link_mat, values_in, adjoint):
    real_rows = []
    imag_rows = []
    for out_row in range(3):
        real_sum = jnp.zeros(values_in.shape[1:2] + values_in.shape[3:], jnp.float32)
        imag_sum = jnp.zeros(values_in.shape[1:2] + values_in.shape[3:], jnp.float32)
        for in_col in range(3):
            if adjoint:
                link_entry = link_mat[in_col, out_row]
                conj_sign = -1.0
            else:
                link_entry = link_mat[out_row, in_col]
                conj_sign = 1.0
            link_real = link_entry[0].astype(jnp.float32)[None]
            link_imag = (conj_sign * link_entry[1].astype(jnp.float32))[None]
            vec_real = values_in[0, :, in_col].astype(jnp.float32)
            vec_imag = values_in[1, :, in_col].astype(jnp.float32)
            real_sum = real_sum + link_real * vec_real - link_imag * vec_imag
            imag_sum = imag_sum + link_real * vec_imag + link_imag * vec_real
        real_rows.append(real_sum)
        imag_rows.append(imag_sum)
    return jnp.stack([jnp.stack(real_rows, axis=1), jnp.stack(imag_rows, axis=1)])


def contract(left, right):
    return lax.dot_general(
        left, right, (((1,), (1,)), ((), ())), preferred_element_type=jnp.float32
    )


def elemental(eigen_field, derivative):
    vectors = eigen_field.shape[1]
    vec_real = eigen_field[0].reshape(vectors, -1)
    vec_imag = eigen_field[1].reshape(vectors, -1)
    der_real = derivative[0].reshape(vectors, -1)
    der_imag = derivative[1].reshape(vectors, -1)
    return jnp.stack(
        [
            contract(vec_real, der_real) + contract(vec_imag, der_imag),
            contract(vec_real, der_imag) - contract(vec_imag, der_real),
        ]
    )


def lattice(values):
    return values.reshape(values.shape[:-1] + (values.shape[-1] // (LX * LZ), LX, LZ))


def general(eigvecs, links, dirs, peram):
    eig_lat = lattice(eigvecs)
    link_lat = lattice(links)
    slab_rows = eig_lat.shape[4]
    back_y = jnp.stack([link_apply(link_lat[0, 1], eig_lat[0], True).astype(jnp.bfloat16)])
    y_ahead = from_behind(eig_lat[:, :, :, :, 0], "space", -1)
    y_behind = from_behind(back_y[:, :, :, :, slab_rows - 1], "space", 1)
    choose = dirs[:, None] == jnp.arange(3, dtype=jnp.int32)[None, :]
    position = 0
    eigen_field = eig_lat[position]
    link_set = link_lat[position]
    elementals = []
    for direction in range(3):
        if direction == 0:
            ahead_field = jnp.roll(eigen_field, -1, axis=4)
            back_term = link_apply(link_set[0], eigen_field, True).astype(jnp.bfloat16)
            behind = jnp.roll(back_term, 1, axis=4)
        elif direction == 1:
            ahead_field = jnp.concatenate(
                [eigen_field[:, :, :, 1:], y_ahead[position][:, :, :, None]], axis=3
            )
            behind = jnp.concatenate(
                [y_behind[position][:, :, :, None], back_y[position][:, :, :, :-1]], axis=3
            )
        else:
            ahead_field = jnp.roll(eigen_field, -1, axis=5)
            back_term = link_apply(link_set[2], eigen_field, True).astype(jnp.bfloat16)
            behind = jnp.roll(back_term, 1, axis=5)
        derivative = (
            link_apply(link_set[direction], ahead_field, False) - behind.astype(jnp.float32)
        ).astype(jnp.bfloat16)
        elementals.append(elemental(eigen_field, derivative))
    elementals = jnp.stack(elementals)
    picked_all = [jnp.sum(jnp.where(choose[:, :, None, None, None], elementals[None], 0.0), axis=1)]
    stacked = jnp.stack(picked_all)
    elem_low = lax.psum(stacked, "space").astype(jnp.bfloat16)
    return finish(elem_low, from_behind(peram, "tm", -1))


def finish(elem_low, blocks):
    columns = blocks.shape[2]
    position = 0
    elem_real = elem_low[position, :, 0]
    elem_imag = elem_low[position, :, 1]
    peram_real = blocks[position, 0].reshape(columns, K, SPIN)
    peram_imag = blocks[position, 1].reshape(columns, K, SPIN)
    out_real = jnp.einsum(
        "jkl,cls->jcks", elem_real, peram_real, preferred_element_type=jnp.float32
    ) - jnp.einsum("jkl,cls->jcks", elem_imag, peram_imag, preferred_element_type=jnp.float32)
    out_imag = jnp.einsum(
        "jkl,cls->jcks", elem_real, peram_imag, preferred_element_type=jnp.float32
    ) + jnp.einsum("jkl,cls->jcks", elem_imag, peram_real, preferred_element_type=jnp.float32)
    combined = jnp.stack([out_real, out_imag], axis=1)
    results = [combined.reshape(combined.shape[0], 2, columns, K * SPIN).astype(jnp.bfloat16)]
    return jnp.stack(results)


def halo_plan(eigvecs):
    n = lax.axis_size("space")
    return (
        eigvecs.shape[-1] == LX * LZ
        and lax.axis_size("tm") == 2
        and n > 1
        and eigvecs.shape[0] == 1
        and K % (16 * n) == 0
    )


def mix(link_ref, direction, adjoint, first, count, source, target):
    def block(start, size):
        rows = pl.ds(start, size)
        sites = pl.ds(start + first, size)
        vec = [[source(ri, c, rows).astype(jnp.float32) for c in range(3)] for ri in range(2)]
        for out_row in range(3):
            real_sum = None
            for in_col in range(3):
                a, b = (in_col, out_row) if adjoint else (out_row, in_col)
                at = ((direction * 3 + a) * 3 + b) * 2
                link_real = link_ref[sites, at : at + 1]
                link_imag = link_ref[sites, at + 1 : at + 2]
                rr = link_real * vec[0][in_col]
                ii = link_imag * vec[1][in_col]
                ri = link_real * vec[1][in_col]
                ir = link_imag * vec[0][in_col]
                real = rr + ii if adjoint else rr - ii
                imag = ri - ir if adjoint else ri + ir
                real_sum = real if real_sum is None else real_sum + real
                imag_sum = imag if in_col == 0 else imag_sum + imag
            target[0, out_row, rows, :] = real_sum.astype(jnp.bfloat16)
            target[1, out_row, rows, :] = imag_sum.astype(jnp.bfloat16)

    @pl.loop(0, count // 16)
    def _(step):
        block(pl.multiple_of(step * 16, 16), 16)

    if count % 16:
        block(count - count % 16, count % 16)


def meet(left, right):
    return lax.dot_general(
        left, right, (((0,), (0,)), ((), ())), preferred_element_type=jnp.float32
    )


def overlap(left, right):
    real = imag = None
    for c in range(3):
        lr, li, rr, ri = left(0, c), left(1, c), right(0, c), right(1, c)
        re = meet(lr, rr) + meet(li, ri)
        im = meet(lr, ri) - meet(li, rr)
        real = re if real is None else real + re
        imag = im if imag is None else imag + im
    return real, imag


def halo_kernel(
    n, v_ref, link_ref, perm_ref, peram_ref, elem_ref, spread_ref,
    shifted, mixed, mixed_lo, up_out, up_in, down_in, part, gathered, low, landed, swapped,
    halo_send, halo_recv, rs_send, rs_recv, ag_send, ag_recv,
):
    me = lax.axis_index("space")
    core = lax.axis_index("tm")
    chunk = K // n
    sites = LX * LZ
    split = upper_rows(sites)

    barrier = pltpu.get_barrier_semaphore()
    for o in range(1, n):
        pl.semaphore_signal(
            barrier, inc=1, device_id={"space": lax.rem(me + o, n)}, device_id_type=MESH
        )
    pl.semaphore_signal(barrier, inc=1, device_id={"tm": 1 - core}, device_id_type=MESH)
    pl.semaphore_wait(barrier, n)

    down = pltpu.make_async_remote_copy(
        src_ref=v_ref.at[:, :, pl.ds(0, split)],
        dst_ref=down_in,
        send_sem=halo_send.at[0],
        recv_sem=halo_recv.at[0],
        device_id={"space": lax.rem(me + n - 1, n)},
        device_id_type=MESH,
    )
    down.start()
    mix(
        link_ref, 1, True, split, sites - split,
        lambda ri, c, rows: v_ref[ri, c, pl.ds(rows.start + split, rows.size)], up_out,
    )
    up = pltpu.make_async_remote_copy(
        src_ref=up_out,
        dst_ref=up_in,
        send_sem=halo_send.at[1],
        recv_sem=halo_recv.at[1],
        device_id={"space": lax.rem(me + 1, n)},
        device_id_type=MESH,
    )
    up.start()
    swap = pltpu.make_async_remote_copy(
        src_ref=peram_ref,
        dst_ref=swapped,
        send_sem=halo_send.at[2],
        recv_sem=halo_recv.at[2],
        device_id={"tm": 1 - core},
        device_id_type=MESH,
    )
    swap.start()

    row = lax.broadcasted_iota(jnp.int32, (K, K), 0)
    col = lax.broadcasted_iota(jnp.int32, (K, K), 1)

    def scatter(direction, real, imag):
        turned = jnp.where(row > col, -real, imag).T
        part[direction] = (jnp.where(row < col, real, imag) + turned).astype(jnp.bfloat16)
        copies = []
        for o in range(1, n):
            peer = lax.rem(me + o, n)
            copy = pltpu.make_async_remote_copy(
                src_ref=part.at[direction, pl.ds(pl.multiple_of(peer * chunk, chunk), chunk)],
                dst_ref=landed.at[direction, o],
                send_sem=rs_send.at[direction, o],
                recv_sem=rs_recv.at[direction, o],
                device_id={"space": peer},
                device_id_type=MESH,
            )
            copy.start()
            copies.append(copy)
        return copies

    def gather(direction, copies):
        mine = pl.ds(pl.multiple_of(me * chunk, chunk), chunk)
        total = part[direction, mine].astype(jnp.float32)
        for o in range(1, n):
            copies[o - 1].wait_recv()
            total = total + landed[direction, o].astype(jnp.float32)
        low[direction] = total.astype(jnp.bfloat16)
        gathered[direction, mine] = low[direction]
        sends = []
        for o in range(1, n):
            copy = pltpu.make_async_remote_copy(
                src_ref=low.at[direction],
                dst_ref=gathered.at[direction, mine],
                send_sem=ag_send.at[direction, o],
                recv_sem=ag_recv.at[direction, o],
                device_id={"space": lax.rem(me + o, n)},
                device_id_type=MESH,
            )
            copy.start()
            sends.append(copy)
        return sends

    def keep(direction, sends):
        for copy in sends:
            copy.wait_recv()
        elem_ref[direction] = gathered[direction]

    own = lambda ri, c: v_ref[ri, c]
    scattered, sent = {}, {}
    for direction, which in ((0, 0), (2, 1)):
        for ri in range(2):
            for c in range(3):
                shifted[ri, c] = jnp.dot(
                    perm_ref[which], v_ref[ri, c], preferred_element_type=jnp.float32
                ).astype(jnp.bfloat16)
        mix(link_ref, direction, False, 0, sites, lambda ri, c, rows: shifted[ri, c, rows], mixed)
        scattered[direction] = scatter(direction, *overlap(own, lambda ri, c: mixed[ri, c]))

    swap.wait()
    order = spin_order(True)
    columns = swapped.shape[1]
    for ri in range(2):
        for b in range(SPIN):
            sorted_block = jnp.dot(
                swapped[ri, :, b * K : (b + 1) * K], order, preferred_element_type=jnp.float32
            ).astype(jnp.bfloat16)
            for spin in range(SPIN):
                at = ri * K + b * (K // SPIN)
                spread_ref[spin * columns : (spin + 1) * columns, at : at + K // SPIN] = sorted_block[
                    :, spin * (K // SPIN) : (spin + 1) * (K // SPIN)
                ]
    for direction in (0, 2):
        sent[direction] = gather(direction, scattered[direction])

    down.wait_recv()
    mix(link_ref, 1, False, 0, split, lambda ri, c, rows: down_in[ri, c, rows], mixed_lo)
    real, imag = overlap(lambda ri, c: v_ref[ri, c, 0:split], lambda ri, c: mixed_lo[ri, c])
    up.wait_recv()
    real_up, imag_up = overlap(lambda ri, c: up_in[ri, c], lambda ri, c: v_ref[ri, c, split:sites])
    scattered[1] = scatter(1, real + real_up, imag + imag_up)
    for direction in (0, 2):
        keep(direction, sent[direction])
    sent[1] = gather(1, scattered[1])
    keep(1, sent[1])
    down.wait_send()
    up.wait_send()
    for direction in range(3):
        for copy in scattered[direction] + sent[direction]:
            copy.wait_send()


def spin_order(apart):
    near = lax.broadcasted_iota(jnp.int32, (K, K), 0 if apart else 1)
    far = lax.broadcasted_iota(jnp.int32, (K, K), 1 if apart else 0)
    part = K // SPIN
    spin = near & (SPIN - 1)
    hit = far * SPIN == spin * (part * SPIN - 1) + near
    return jnp.where(hit, 1.0, 0.0).astype(jnp.bfloat16)


def upper_rows(sites):
    return (sites + 31) // 32 * 16


def finish_kernel(dirs_ref, elem_ref, spread_ref, out_ref):
    columns = out_ref.shape[2]
    part = K // SPIN
    row = lax.broadcasted_iota(jnp.int32, (K, K), 0)
    col = lax.broadcasted_iota(jnp.int32, (K, K), 1)
    back = spin_order(False)
    packed = elem_ref[dirs_ref[pl.program_id(0)]].astype(jnp.float32)
    flipped = packed.T
    minus_real = jnp.where(row < col, -packed, jnp.where(row > col, flipped, 0.0)).astype(jnp.bfloat16)
    imag = jnp.where(row < col, flipped, packed)
    minus_imag = (-imag).astype(jnp.bfloat16)
    imag = imag.astype(jnp.bfloat16)
    for ri, (first, second) in enumerate(((minus_real, minus_imag), (imag, minus_real))):
        result = jnp.dot(
            spread_ref[...], jnp.concatenate([first, second], axis=0), preferred_element_type=jnp.float32
        ).astype(jnp.bfloat16)
        for b in range(SPIN):
            block = jnp.concatenate(
                [
                    result[spin * columns : (spin + 1) * columns, b * part : (b + 1) * part]
                    for spin in range(SPIN)
                ],
                axis=1,
            )
            out_ref[0, ri, :, b * K : (b + 1) * K] = jnp.dot(
                block, back, preferred_element_type=jnp.float32
            ).astype(jnp.bfloat16)


def finish_packed(dirs, elem, spread, columns):
    return pl.pallas_call(
        finish_kernel,
        grid=(3,),
        out_shape=jax.ShapeDtypeStruct((3, 2, columns, K * SPIN), jnp.bfloat16),
        in_specs=[
            pl.BlockSpec(memory_space=pltpu.SMEM),
            pl.BlockSpec((3, K, K), lambda j: (0, 0, 0)),
            pl.BlockSpec((SPIN * columns, 2 * K), lambda j: (0, 0)),
        ],
        out_specs=pl.BlockSpec((1, 2, columns, K * SPIN), lambda j: (j, 0, 0, 0)),
        compiler_params=pltpu.CompilerParams(vmem_limit_bytes=40 * 2**20),
    )(dirs, elem, spread)


def shift_tables():
    site = np.arange(LX * LZ)
    x, z = site // LZ, site % LZ
    tables = []
    for source in (((x + 1) % LX) * LZ + z, x * LZ + (z + 1) % LZ):
        tables.append(source[:, None] == site[None, :])
    return jnp.asarray(np.stack(tables), jnp.bfloat16)


def exchange(eigvecs, links, peram):
    n = lax.axis_size("space")
    sites = LX * LZ
    split = upper_rows(sites)
    columns = peram.shape[2]
    bf, chunk = jnp.bfloat16, K // n
    vmem = pl.BlockSpec(memory_space=pltpu.VMEM)
    return pl.pallas_call(
        functools.partial(halo_kernel, n),
        out_shape=(
            jax.ShapeDtypeStruct((3, K, K), bf),
            jax.ShapeDtypeStruct((SPIN * columns, 2 * K), bf),
        ),
        in_specs=[vmem] * 4,
        out_specs=(vmem, vmem),
        scratch_shapes=[
            pltpu.VMEM((2, 3, sites, K), bf),
            pltpu.VMEM((2, 3, sites, K), bf),
            pltpu.VMEM((2, 3, split, K), bf),
            pltpu.VMEM((2, 3, sites - split, K), bf),
            pltpu.VMEM((2, 3, sites - split, K), bf),
            pltpu.VMEM((2, 3, split, K), bf),
            pltpu.VMEM((3, K, K), bf),
            pltpu.VMEM((3, K, K), bf),
            pltpu.VMEM((3, chunk, K), bf),
            pltpu.VMEM((3, n, chunk, K), bf),
            pltpu.VMEM(peram.shape[1:], bf),
            pltpu.SemaphoreType.DMA((3,)),
            pltpu.SemaphoreType.DMA((3,)),
            pltpu.SemaphoreType.DMA((3, n)),
            pltpu.SemaphoreType.DMA((3, n)),
            pltpu.SemaphoreType.DMA((3, n)),
            pltpu.SemaphoreType.DMA((3, n)),
        ],
        compiler_params=pltpu.CompilerParams(
            collective_id=0, has_side_effects=True, vmem_limit_bytes=40 * 2**20
        ),
    )(
        jnp.transpose(eigvecs[0], (0, 2, 3, 1)),
        links[0].reshape(54, sites).T.astype(jnp.float32),
        shift_tables(),
        peram[0],
    )


def on_device(eigvecs, links, dirs, peram):
    if halo_plan(eigvecs):
        elem, spread = exchange(eigvecs, links, peram)
        return finish_packed(dirs, elem, spread, peram.shape[2])[None]
    return general(eigvecs, links, dirs, peram)


def solution(mesh):
    placed = (
        P(("parts", "tm"), None, None, None, "space"),
        P(("parts", "tm"), None, None, None, None, "space"),
        P(),
        P(("parts", "tm"), None, "space", None),
    )
    return jax.shard_map(
        on_device,
        mesh=mesh,
        in_specs=placed,
        out_specs=P(("parts", "tm"), None, None, "space", None),
        check_vma=False,
    )
```

```python
import functools

import jax
import jax.numpy as jnp
from jax import lax
from jax.experimental import pallas as pl
from jax.experimental.pallas import tpu as pltpu
from jax.sharding import PartitionSpec as P

K = 256
SPIN = 4
LX = 9
LZ = 24
MESH = pl.DeviceIdType.MESH


def from_behind(block, axis, distance):
    devices = range(lax.axis_size(axis))
    route = [((i - distance) % len(devices), i) for i in devices]
    return lax.ppermute(block, axis, route)


def link_apply(link_mat, values_in, adjoint):
    real_rows = []
    imag_rows = []
    for out_row in range(3):
        real_sum = jnp.zeros(values_in.shape[1:2] + values_in.shape[3:], jnp.float32)
        imag_sum = jnp.zeros(values_in.shape[1:2] + values_in.shape[3:], jnp.float32)
        for in_col in range(3):
            if adjoint:
                link_entry = link_mat[in_col, out_row]
                conj_sign = -1.0
            else:
                link_entry = link_mat[out_row, in_col]
                conj_sign = 1.0
            link_real = link_entry[0].astype(jnp.float32)[None]
            link_imag = (conj_sign * link_entry[1].astype(jnp.float32))[None]
            vec_real = values_in[0, :, in_col].astype(jnp.float32)
            vec_imag = values_in[1, :, in_col].astype(jnp.float32)
            real_sum = real_sum + link_real * vec_real - link_imag * vec_imag
            imag_sum = imag_sum + link_real * vec_imag + link_imag * vec_real
        real_rows.append(real_sum)
        imag_rows.append(imag_sum)
    return jnp.stack([jnp.stack(real_rows, axis=1), jnp.stack(imag_rows, axis=1)])


def contract(left, right):
    return lax.dot_general(
        left, right, (((1,), (1,)), ((), ())), preferred_element_type=jnp.float32
    )


def elemental(eigen_field, derivative):
    vectors = eigen_field.shape[1]
    vec_real = eigen_field[0].reshape(vectors, -1)
    vec_imag = eigen_field[1].reshape(vectors, -1)
    der_real = derivative[0].reshape(vectors, -1)
    der_imag = derivative[1].reshape(vectors, -1)
    return jnp.stack(
        [
            contract(vec_real, der_real) + contract(vec_imag, der_imag),
            contract(vec_real, der_imag) - contract(vec_imag, der_real),
        ]
    )


def lattice(values):
    return values.reshape(values.shape[:-1] + (values.shape[-1] // (LX * LZ), LX, LZ))


def general(eigvecs, links, dirs, peram):
    eig_lat = lattice(eigvecs)
    link_lat = lattice(links)
    slab_rows = eig_lat.shape[4]
    back_y = jnp.stack([link_apply(link_lat[0, 1], eig_lat[0], True).astype(jnp.bfloat16)])
    y_ahead = from_behind(eig_lat[:, :, :, :, 0], "space", -1)
    y_behind = from_behind(back_y[:, :, :, :, slab_rows - 1], "space", 1)
    choose = dirs[:, None] == jnp.arange(3, dtype=jnp.int32)[None, :]
    position = 0
    eigen_field = eig_lat[position]
    link_set = link_lat[position]
    elementals = []
    for direction in range(3):
        if direction == 0:
            ahead_field = jnp.roll(eigen_field, -1, axis=4)
            back_term = link_apply(link_set[0], eigen_field, True).astype(jnp.bfloat16)
            behind = jnp.roll(back_term, 1, axis=4)
        elif direction == 1:
            ahead_field = jnp.concatenate(
                [eigen_field[:, :, :, 1:], y_ahead[position][:, :, :, None]], axis=3
            )
            behind = jnp.concatenate(
                [y_behind[position][:, :, :, None], back_y[position][:, :, :, :-1]], axis=3
            )
        else:
            ahead_field = jnp.roll(eigen_field, -1, axis=5)
            back_term = link_apply(link_set[2], eigen_field, True).astype(jnp.bfloat16)
            behind = jnp.roll(back_term, 1, axis=5)
        derivative = (
            link_apply(link_set[direction], ahead_field, False) - behind.astype(jnp.float32)
        ).astype(jnp.bfloat16)
        elementals.append(elemental(eigen_field, derivative))
    elementals = jnp.stack(elementals)
    picked_all = [jnp.sum(jnp.where(choose[:, :, None, None, None], elementals[None], 0.0), axis=1)]
    stacked = jnp.stack(picked_all)
    elem_low = lax.psum(stacked, "space").astype(jnp.bfloat16)
    return finish(elem_low, from_behind(peram, "tm", -1))


def finish(elem_low, blocks):
    columns = blocks.shape[2]
    position = 0
    elem_real = elem_low[position, :, 0]
    elem_imag = elem_low[position, :, 1]
    peram_real = blocks[position, 0].reshape(columns, K, SPIN)
    peram_imag = blocks[position, 1].reshape(columns, K, SPIN)
    out_real = jnp.einsum(
        "jkl,cls->jcks", elem_real, peram_real, preferred_element_type=jnp.float32
    ) - jnp.einsum("jkl,cls->jcks", elem_imag, peram_imag, preferred_element_type=jnp.float32)
    out_imag = jnp.einsum(
        "jkl,cls->jcks", elem_real, peram_imag, preferred_element_type=jnp.float32
    ) + jnp.einsum("jkl,cls->jcks", elem_imag, peram_real, preferred_element_type=jnp.float32)
    combined = jnp.stack([out_real, out_imag], axis=1)
    results = [combined.reshape(combined.shape[0], 2, columns, K * SPIN).astype(jnp.bfloat16)]
    return jnp.stack(results)


def halo_plan(eigvecs):
    n = lax.axis_size("space")
    return (
        eigvecs.shape[-1] == LX * LZ
        and lax.axis_size("tm") == 2
        and n % 2 == 0
        and eigvecs.shape[0] == 1
        and K % (16 * n) == 0
    )


def mix(link_ref, direction, adjoint, first, count, source, target):
    def block(start, size):
        rows = pl.ds(start, size)
        sites = pl.ds(start + first, size)
        vec = [[source(ri, c, rows).astype(jnp.float32) for c in range(3)] for ri in range(2)]
        for out_row in range(3):
            real_sum = None
            for in_col in range(3):
                a, b = (in_col, out_row) if adjoint else (out_row, in_col)
                at = ((direction * 3 + a) * 3 + b) * 2
                link_real = link_ref[sites, at : at + 1]
                link_imag = link_ref[sites, at + 1 : at + 2]
                rr = link_real * vec[0][in_col]
                ii = link_imag * vec[1][in_col]
                ri = link_real * vec[1][in_col]
                ir = link_imag * vec[0][in_col]
                real = rr + ii if adjoint else rr - ii
                imag = ri - ir if adjoint else ri + ir
                real_sum = real if real_sum is None else real_sum + real
                imag_sum = imag if in_col == 0 else imag_sum + imag
            target[0, out_row, rows, :] = real_sum.astype(jnp.bfloat16)
            target[1, out_row, rows, :] = imag_sum.astype(jnp.bfloat16)

    @pl.loop(0, count // 16)
    def _(step):
        block(pl.multiple_of(step * 16, 16), 16)

    if count % 16:
        block(count - count % 16, count % 16)


def meet(left, right):
    return lax.dot_general(
        left, right, (((0,), (0,)), ((), ())), preferred_element_type=jnp.float32
    )


def overlap(left, right):
    real = imag = None
    for c in range(3):
        lr, li, rr, ri = left(0, c), left(1, c), right(0, c), right(1, c)
        re = meet(lr, rr) + meet(li, ri)
        im = meet(lr, ri) - meet(li, rr)
        real = re if real is None else real + re
        imag = im if imag is None else imag + im
    return real, imag


def halo_kernel(
    n, v_hbm, link_ref, peram_hbm, elem_ref, spread_ref, v_ref, tables,
    shifted, mixed, mixed_lo, up_out, up_in, down_in, part, gathered, low, landed, landed_levels, landed_pair, quarters, swapped,
    load_sem, halo_send, halo_recv, rs_send, rs_recv, ag_send, ag_recv,
):
    me = lax.axis_index("space")
    core = lax.axis_index("tm")
    chunk = K // n
    sites = LX * LZ
    split = upper_rows(sites)

    load = pltpu.make_async_copy(v_hbm, v_ref, load_sem)
    load.start()
    barrier = pltpu.get_barrier_semaphore()
    for o in range(1, n):
        pl.semaphore_signal(
            barrier, inc=1, device_id={"space": lax.rem(me + o, n)}, device_id_type=MESH
        )
    pl.semaphore_signal(barrier, inc=1, device_id={"tm": 1 - core}, device_id_type=MESH)
    pl.semaphore_wait(barrier, n)

    down = pltpu.make_async_remote_copy(
        src_ref=v_hbm.at[:, :, pl.ds(0, split)],
        dst_ref=down_in,
        send_sem=halo_send.at[0],
        recv_sem=halo_recv.at[0],
        device_id={"space": lax.rem(me + n - 1, n)},
        device_id_type=MESH,
    )
    down.start()
    load.wait()
    mix(
        link_ref, 1, True, split, sites - split,
        lambda ri, c, rows: v_ref[ri, c, pl.ds(rows.start + split, rows.size)], up_out,
    )
    up = pltpu.make_async_remote_copy(
        src_ref=up_out,
        dst_ref=up_in,
        send_sem=halo_send.at[1],
        recv_sem=halo_recv.at[1],
        device_id={"space": lax.rem(me + 1, n)},
        device_id_type=MESH,
    )
    up.start()
    swap = pltpu.make_async_remote_copy(
        src_ref=peram_hbm,
        dst_ref=swapped,
        send_sem=halo_send.at[2],
        recv_sem=halo_recv.at[2],
        device_id={"tm": 1 - core},
        device_id_type=MESH,
    )
    swap.start()

    row = lax.broadcasted_iota(jnp.int32, (K, K), 0)
    col = lax.broadcasted_iota(jnp.int32, (K, K), 1)

    half = lax.rem(me, 2)
    level = lax.div(me, 2)
    levels = n // 2
    pair = me + 1 - 2 * half
    quarter = 2 * chunk

    def send(src, dst, out_sem, in_sem, peer):
        copy = pltpu.make_async_remote_copy(
            src_ref=src, dst_ref=dst, send_sem=out_sem, recv_sem=in_sem,
            device_id={"space": peer}, device_id_type=MESH,
        )
        copy.start()
        return copy

    def band(index, size):
        return pl.ds(pl.multiple_of(index * size, size), size)

    def pack(direction, real, imag):
        turned = jnp.where(row > col, -real, imag).T
        part[direction] = (jnp.where(row < col, real, imag) + turned).astype(jnp.bfloat16)

    def scatter(direction):
        copies = []
        for o in range(1, n):
            peer = lax.rem(me + o, n)
            copies.append(send(
                part.at[direction, band(peer, chunk)], landed.at[o],
                rs_send.at[direction, o], rs_recv.at[direction, o], peer,
            ))
        return copies

    def gather(direction, copies):
        total = part[direction, band(me, chunk)].astype(jnp.float32)
        for o in range(1, n):
            copies[o - 1].wait_recv()
            total = total + landed[o].astype(jnp.float32)
        low[direction] = total.astype(jnp.bfloat16)
        gathered[direction, band(me, chunk)] = low[direction]
        return [
            send(
                low.at[direction], gathered.at[direction, band(me, chunk)],
                ag_send.at[direction, o], ag_recv.at[direction, o], lax.rem(me + o, n),
            )
            for o in range(1, n)
        ]

    def level_peer(o):
        to = lax.rem(level + o, levels)
        return to, to * 2 + half

    def scatter_levels(direction):
        copies = []
        for o in range(1, levels):
            to, peer = level_peer(o)
            copies.append(send(
                part.at[direction, band(to, quarter)], landed_levels.at[direction, o],
                rs_send.at[direction, o], rs_recv.at[direction, o], peer,
            ))
        return copies

    def scatter_pair(direction, copies):
        total = part[direction, band(level, quarter)].astype(jnp.float32)
        for o in range(1, levels):
            copies[o - 1].wait_recv()
            total = total + landed_levels[direction, o].astype(jnp.float32)
        quarters[direction] = total.astype(jnp.bfloat16)
        return send(
            quarters.at[direction, band(1 - half, chunk)], landed_pair.at[direction],
            rs_send.at[direction, 0], rs_recv.at[direction, 0], pair,
        )

    def gather_levels(direction, copy):
        copy.wait_recv()
        total = quarters[direction, band(half, chunk)].astype(jnp.float32)
        low[direction] = (total + landed_pair[direction].astype(jnp.float32)).astype(jnp.bfloat16)
        gathered[direction, band(me, chunk)] = low[direction]
        copies = [send(
            low.at[direction], gathered.at[direction, band(me, chunk)],
            ag_send.at[direction, 0], ag_recv.at[direction, 0], pair,
        )]
        for o in range(1, levels):
            copies.append(send(
                low.at[direction], gathered.at[direction, band(me, chunk)],
                ag_send.at[direction, o], ag_recv.at[direction, o], level_peer(o)[1],
            ))
        return copies

    def gather_pair(direction, copies):
        passed = []
        for o in range(1, levels):
            copies[o].wait_recv()
            rows = band(lax.rem(level - o + levels, levels) * 2 + half, chunk)
            passed.append(send(
                gathered.at[direction, rows], gathered.at[direction, rows],
                ag_send.at[direction, levels + o], ag_recv.at[direction, levels + o], pair,
            ))
        return copies[:1] + passed

    def keep(direction, sends):
        for copy in sends:
            copy.wait_recv()
        packed = gathered[direction].astype(jnp.float32)
        flipped = packed.T
        upper = row < col
        minus_real = jnp.where(upper, -packed, jnp.where(row > col, flipped, 0.0)).astype(jnp.bfloat16)
        imag = jnp.where(upper, flipped, packed)
        elem_ref[direction, 0:K, 0:K] = minus_real
        elem_ref[direction, K : 2 * K, K : 2 * K] = minus_real
        elem_ref[direction, 0:K, K : 2 * K] = imag.astype(jnp.bfloat16)
        elem_ref[direction, K : 2 * K, 0:K] = (-imag).astype(jnp.bfloat16)

    own = lambda ri, c: v_ref[ri, c]
    shift_tables(tables, sites)
    first = {}
    for direction, which in ((0, 0), (2, 1)):
        for ri in range(2):
            for c in range(3):
                shifted[ri, c] = jnp.dot(
                    tables[which], v_ref[ri, c], preferred_element_type=jnp.float32
                ).astype(jnp.bfloat16)
        mix(link_ref, direction, False, 0, sites, lambda ri, c, rows: shifted[ri, c, rows], mixed)
        pack(direction, *overlap(own, lambda ri, c: mixed[ri, c]))
        first[direction] = scatter_levels(direction)

    swap.wait()
    order = spin_order(True)
    columns = swapped.shape[1]
    for ri in range(2):
        for b in range(SPIN):
            sorted_block = jnp.dot(
                swapped[ri, :, b * K : (b + 1) * K], order, preferred_element_type=jnp.float32
            ).astype(jnp.bfloat16)
            for spin in range(SPIN):
                at = ri * K + b * (K // SPIN)
                spread_ref[spin * columns : (spin + 1) * columns, at : at + K // SPIN] = sorted_block[
                    :, spin * (K // SPIN) : (spin + 1) * (K // SPIN)
                ]
    second = {direction: scatter_pair(direction, first[direction]) for direction in (0, 2)}

    down.wait_recv()
    mix(link_ref, 1, False, 0, split, lambda ri, c, rows: down_in[ri, c, rows], mixed_lo)
    real, imag = overlap(lambda ri, c: v_ref[ri, c, 0:split], lambda ri, c: mixed_lo[ri, c])
    third = {direction: gather_levels(direction, second[direction]) for direction in (0, 2)}
    up.wait_recv()
    real_up, imag_up = overlap(lambda ri, c: up_in[ri, c], lambda ri, c: v_ref[ri, c, split:sites])
    pack(1, real + real_up, imag + imag_up)
    scattered = scatter(1)
    last = {direction: gather_pair(direction, third[direction]) for direction in (0, 2)}
    sent = gather(1, scattered)
    for direction in (0, 2):
        keep(direction, last[direction])
    keep(1, sent)
    down.wait_send()
    up.wait_send()
    for copy in scattered + sent:
        copy.wait_send()
    for direction in (0, 2):
        for copy in first[direction] + [second[direction]] + third[direction] + last[direction][1:]:
            copy.wait_send()


def spin_order(apart):
    near = lax.broadcasted_iota(jnp.int32, (K, K), 0 if apart else 1)
    far = lax.broadcasted_iota(jnp.int32, (K, K), 1 if apart else 0)
    part = K // SPIN
    spin = near & (SPIN - 1)
    hit = far * SPIN == spin * (part * SPIN - 1) + near
    return jnp.where(hit, 1.0, 0.0).astype(jnp.bfloat16)


def upper_rows(sites):
    return (sites + 31) // 32 * 16


def finish_kernel(dirs_ref, elem_ref, spread_ref, out_ref):
    columns = out_ref.shape[2]
    part = K // SPIN
    back = spin_order(False)
    result = jnp.dot(
        spread_ref[...], elem_ref[dirs_ref[pl.program_id(0)]], preferred_element_type=jnp.float32
    ).astype(jnp.bfloat16)
    stacked = jnp.concatenate(
        [
            jnp.concatenate(
                [
                    result[s * columns : (s + 1) * columns, ri * K + b * part : ri * K + (b + 1) * part]
                    for s in range(SPIN)
                ],
                axis=1,
            )
            for ri in range(2)
            for b in range(SPIN)
        ],
        axis=0,
    )
    mixed = jnp.dot(stacked, back, preferred_element_type=jnp.float32).astype(jnp.bfloat16)
    for ri in range(2):
        for b in range(SPIN):
            at = (ri * SPIN + b) * columns
            out_ref[0, ri, :, b * K : (b + 1) * K] = mixed[at : at + columns]


def finish_packed(dirs, elem, spread, columns):
    return pl.pallas_call(
        finish_kernel,
        grid=(3,),
        out_shape=jax.ShapeDtypeStruct((3, 2, columns, K * SPIN), jnp.bfloat16),
        in_specs=[
            pl.BlockSpec(memory_space=pltpu.SMEM),
            pl.BlockSpec(memory_space=pltpu.VMEM),
            pl.BlockSpec(memory_space=pltpu.VMEM),
        ],
        out_specs=pl.BlockSpec((1, 2, columns, K * SPIN), lambda j: (j, 0, 0, 0)),
        compiler_params=pltpu.CompilerParams(vmem_limit_bytes=40 * 2**20),
    )(dirs, elem, spread)


def shift_tables(tables, sites):
    here = lax.broadcasted_iota(jnp.int32, (sites, sites), 0)
    there = lax.broadcasted_iota(jnp.int32, (sites, sites), 1)
    step = there - here
    tables[0] = jnp.where((step == LZ) | (step == LZ - sites), 1.0, 0.0).astype(jnp.bfloat16)
    first = there == 0
    for x in range(1, LX):
        first = first | (there == x * LZ)
    wanted = jnp.where(first, 1 - LZ, 1)
    tables[1] = jnp.where(step == wanted, 1.0, 0.0).astype(jnp.bfloat16)


def exchange(eigvecs, links, peram):
    n = lax.axis_size("space")
    sites = LX * LZ
    split = upper_rows(sites)
    columns = peram.shape[2]
    bf, chunk = jnp.bfloat16, K // n
    vmem = pl.BlockSpec(memory_space=pltpu.VMEM)
    hbm = pl.BlockSpec(memory_space=pltpu.HBM)
    return pl.pallas_call(
        functools.partial(halo_kernel, n),
        out_shape=(
            jax.ShapeDtypeStruct((3, 2 * K, 2 * K), bf),
            jax.ShapeDtypeStruct((SPIN * columns, 2 * K), bf),
        ),
        in_specs=[hbm, vmem, hbm],
        out_specs=(vmem, vmem),
        scratch_shapes=[
            pltpu.VMEM((2, 3, sites, K), bf),
            pltpu.VMEM((2, sites, sites), bf),
            pltpu.VMEM((2, 3, sites, K), bf),
            pltpu.VMEM((2, 3, sites, K), bf),
            pltpu.VMEM((2, 3, split, K), bf),
            pltpu.VMEM((2, 3, sites - split, K), bf),
            pltpu.VMEM((2, 3, sites - split, K), bf),
            pltpu.VMEM((2, 3, split, K), bf),
            pltpu.VMEM((3, K, K), bf),
            pltpu.VMEM((3, K, K), bf),
            pltpu.VMEM((3, chunk, K), bf),
            pltpu.VMEM((n, chunk, K), bf),
            pltpu.VMEM((3, n // 2, 2 * chunk, K), bf),
            pltpu.VMEM((3, chunk, K), bf),
            pltpu.VMEM((3, 2 * chunk, K), bf),
            pltpu.VMEM(peram.shape[1:], bf),
            pltpu.SemaphoreType.DMA,
            pltpu.SemaphoreType.DMA((3,)),
            pltpu.SemaphoreType.DMA((3,)),
            pltpu.SemaphoreType.DMA((3, n)),
            pltpu.SemaphoreType.DMA((3, n)),
            pltpu.SemaphoreType.DMA((3, n)),
            pltpu.SemaphoreType.DMA((3, n)),
        ],
        compiler_params=pltpu.CompilerParams(
            collective_id=0, has_side_effects=True, vmem_limit_bytes=40 * 2**20
        ),
    )(
        jnp.transpose(eigvecs[0], (0, 2, 3, 1)),
        links[0].reshape(54, sites).T.astype(jnp.float32),
        peram[0],
    )


def on_device(eigvecs, links, dirs, peram):
    if halo_plan(eigvecs):
        elem, spread = exchange(eigvecs, links, peram)
        return finish_packed(dirs, elem, spread, peram.shape[2])[None]
    return general(eigvecs, links, dirs, peram)


def solution(mesh):
    placed = (
        P(("parts", "tm"), None, None, None, "space"),
        P(("parts", "tm"), None, None, None, None, "space"),
        P(),
        P(("parts", "tm"), None, "space", None),
    )
    return jax.shard_map(
        on_device,
        mesh=mesh,
        in_specs=placed,
        out_specs=P(("parts", "tm"), None, None, "space", None),
        check_vma=False,
    )
```

```python
import functools

import jax
import jax.numpy as jnp
from jax import lax
from jax.experimental import pallas as pl
from jax.experimental.pallas import tpu as pltpu
from jax.sharding import PartitionSpec as P

K = 256
SPIN = 4
LX = 9
LZ = 24
MESH = pl.DeviceIdType.MESH


def from_behind(block, axis, distance):
    devices = range(lax.axis_size(axis))
    route = [((i - distance) % len(devices), i) for i in devices]
    return lax.ppermute(block, axis, route)


def link_apply(link_mat, values_in, adjoint):
    real_rows = []
    imag_rows = []
    for out_row in range(3):
        real_sum = jnp.zeros(values_in.shape[1:2] + values_in.shape[3:], jnp.float32)
        imag_sum = jnp.zeros(values_in.shape[1:2] + values_in.shape[3:], jnp.float32)
        for in_col in range(3):
            if adjoint:
                link_entry = link_mat[in_col, out_row]
                conj_sign = -1.0
            else:
                link_entry = link_mat[out_row, in_col]
                conj_sign = 1.0
            link_real = link_entry[0].astype(jnp.float32)[None]
            link_imag = (conj_sign * link_entry[1].astype(jnp.float32))[None]
            vec_real = values_in[0, :, in_col].astype(jnp.float32)
            vec_imag = values_in[1, :, in_col].astype(jnp.float32)
            real_sum = real_sum + link_real * vec_real - link_imag * vec_imag
            imag_sum = imag_sum + link_real * vec_imag + link_imag * vec_real
        real_rows.append(real_sum)
        imag_rows.append(imag_sum)
    return jnp.stack([jnp.stack(real_rows, axis=1), jnp.stack(imag_rows, axis=1)])


def contract(left, right):
    return lax.dot_general(
        left, right, (((1,), (1,)), ((), ())), preferred_element_type=jnp.float32
    )


def elemental(eigen_field, derivative):
    vectors = eigen_field.shape[1]
    vec_real = eigen_field[0].reshape(vectors, -1)
    vec_imag = eigen_field[1].reshape(vectors, -1)
    der_real = derivative[0].reshape(vectors, -1)
    der_imag = derivative[1].reshape(vectors, -1)
    return jnp.stack(
        [
            contract(vec_real, der_real) + contract(vec_imag, der_imag),
            contract(vec_real, der_imag) - contract(vec_imag, der_real),
        ]
    )


def lattice(values):
    return values.reshape(values.shape[:-1] + (values.shape[-1] // (LX * LZ), LX, LZ))


def general(eigvecs, links, dirs, peram):
    eig_lat = lattice(eigvecs)
    link_lat = lattice(links)
    slab_rows = eig_lat.shape[4]
    back_y = jnp.stack([link_apply(link_lat[0, 1], eig_lat[0], True).astype(jnp.bfloat16)])
    y_ahead = from_behind(eig_lat[:, :, :, :, 0], "space", -1)
    y_behind = from_behind(back_y[:, :, :, :, slab_rows - 1], "space", 1)
    choose = dirs[:, None] == jnp.arange(3, dtype=jnp.int32)[None, :]
    position = 0
    eigen_field = eig_lat[position]
    link_set = link_lat[position]
    elementals = []
    for direction in range(3):
        if direction == 0:
            ahead_field = jnp.roll(eigen_field, -1, axis=4)
            back_term = link_apply(link_set[0], eigen_field, True).astype(jnp.bfloat16)
            behind = jnp.roll(back_term, 1, axis=4)
        elif direction == 1:
            ahead_field = jnp.concatenate(
                [eigen_field[:, :, :, 1:], y_ahead[position][:, :, :, None]], axis=3
            )
            behind = jnp.concatenate(
                [y_behind[position][:, :, :, None], back_y[position][:, :, :, :-1]], axis=3
            )
        else:
            ahead_field = jnp.roll(eigen_field, -1, axis=5)
            back_term = link_apply(link_set[2], eigen_field, True).astype(jnp.bfloat16)
            behind = jnp.roll(back_term, 1, axis=5)
        derivative = (
            link_apply(link_set[direction], ahead_field, False) - behind.astype(jnp.float32)
        ).astype(jnp.bfloat16)
        elementals.append(elemental(eigen_field, derivative))
    elementals = jnp.stack(elementals)
    picked_all = [jnp.sum(jnp.where(choose[:, :, None, None, None], elementals[None], 0.0), axis=1)]
    stacked = jnp.stack(picked_all)
    elem_low = lax.psum(stacked, "space").astype(jnp.bfloat16)
    return finish(elem_low, from_behind(peram, "tm", -1))


def finish(elem_low, blocks):
    columns = blocks.shape[2]
    position = 0
    elem_real = elem_low[position, :, 0]
    elem_imag = elem_low[position, :, 1]
    peram_real = blocks[position, 0].reshape(columns, K, SPIN)
    peram_imag = blocks[position, 1].reshape(columns, K, SPIN)
    out_real = jnp.einsum(
        "jkl,cls->jcks", elem_real, peram_real, preferred_element_type=jnp.float32
    ) - jnp.einsum("jkl,cls->jcks", elem_imag, peram_imag, preferred_element_type=jnp.float32)
    out_imag = jnp.einsum(
        "jkl,cls->jcks", elem_real, peram_imag, preferred_element_type=jnp.float32
    ) + jnp.einsum("jkl,cls->jcks", elem_imag, peram_real, preferred_element_type=jnp.float32)
    combined = jnp.stack([out_real, out_imag], axis=1)
    results = [combined.reshape(combined.shape[0], 2, columns, K * SPIN).astype(jnp.bfloat16)]
    return jnp.stack(results)


def halo_plan(eigvecs):
    n = lax.axis_size("space")
    return (
        eigvecs.shape[-1] == LX * LZ
        and lax.axis_size("tm") == 2
        and n % 2 == 0
        and eigvecs.shape[0] == 1
        and K % (16 * n) == 0
    )


def mix(link_ref, direction, adjoint, first, count, source, target):
    def block(start, size):
        rows = pl.ds(start, size)
        sites = pl.ds(start + first, size)
        vec = [[source(ri, c, rows).astype(jnp.float32) for c in range(3)] for ri in range(2)]
        for out_row in range(3):
            real_sum = None
            for in_col in range(3):
                a, b = (in_col, out_row) if adjoint else (out_row, in_col)
                at = ((direction * 3 + a) * 3 + b) * 2
                link_real = link_ref[sites, at : at + 1]
                link_imag = link_ref[sites, at + 1 : at + 2]
                rr = link_real * vec[0][in_col]
                ii = link_imag * vec[1][in_col]
                ri = link_real * vec[1][in_col]
                ir = link_imag * vec[0][in_col]
                real = rr + ii if adjoint else rr - ii
                imag = ri - ir if adjoint else ri + ir
                real_sum = real if real_sum is None else real_sum + real
                imag_sum = imag if in_col == 0 else imag_sum + imag
            target[0, out_row, rows, :] = real_sum.astype(jnp.bfloat16)
            target[1, out_row, rows, :] = imag_sum.astype(jnp.bfloat16)

    @pl.loop(0, count // 16)
    def _(step):
        block(pl.multiple_of(step * 16, 16), 16)

    if count % 16:
        block(count - count % 16, count % 16)


def meet(left, right):
    return lax.dot_general(
        left, right, (((0,), (0,)), ((), ())), preferred_element_type=jnp.float32
    )


def overlap(left, right):
    real = imag = None
    for c in range(3):
        lr, li, rr, ri = left(0, c), left(1, c), right(0, c), right(1, c)
        re = meet(lr, rr) + meet(li, ri)
        im = meet(lr, ri) - meet(li, rr)
        real = re if real is None else real + re
        imag = im if imag is None else imag + im
    return real, imag


def halo_kernel(
    n, v_hbm, link_ref, peram_hbm, elem_ref, spread_ref, v_ref, tables,
    shifted, mixed, mixed_lo, up_out, up_in, down_in, part, gathered, low, landed, landed_levels, landed_pair, quarters, swapped,
    load_sem, halo_send, halo_recv, rs_send, rs_recv, ag_send, ag_recv,
):
    me = lax.axis_index("space")
    core = lax.axis_index("tm")
    chunk = K // n
    sites = LX * LZ
    split = upper_rows(sites)

    load = pltpu.make_async_copy(v_hbm, v_ref, load_sem)
    load.start()
    barrier = pltpu.get_barrier_semaphore()
    for o in range(1, n):
        pl.semaphore_signal(
            barrier, inc=1, device_id={"space": lax.rem(me + o, n)}, device_id_type=MESH
        )
    pl.semaphore_signal(barrier, inc=1, device_id={"tm": 1 - core}, device_id_type=MESH)
    load.wait()
    mix(
        link_ref, 1, True, split, sites - split,
        lambda ri, c, rows: v_ref[ri, c, pl.ds(rows.start + split, rows.size)], up_out,
    )
    shift_tables(tables, sites)
    pl.semaphore_wait(barrier, n)

    down = pltpu.make_async_remote_copy(
        src_ref=v_hbm.at[:, :, pl.ds(0, split)],
        dst_ref=down_in,
        send_sem=halo_send.at[0],
        recv_sem=halo_recv.at[0],
        device_id={"space": lax.rem(me + n - 1, n)},
        device_id_type=MESH,
    )
    down.start()
    up = pltpu.make_async_remote_copy(
        src_ref=up_out,
        dst_ref=up_in,
        send_sem=halo_send.at[1],
        recv_sem=halo_recv.at[1],
        device_id={"space": lax.rem(me + 1, n)},
        device_id_type=MESH,
    )
    up.start()
    swap = pltpu.make_async_remote_copy(
        src_ref=peram_hbm,
        dst_ref=swapped,
        send_sem=halo_send.at[2],
        recv_sem=halo_recv.at[2],
        device_id={"tm": 1 - core},
        device_id_type=MESH,
    )
    swap.start()

    row = lax.broadcasted_iota(jnp.int32, (K, K), 0)
    col = lax.broadcasted_iota(jnp.int32, (K, K), 1)

    half = lax.rem(me, 2)
    level = lax.div(me, 2)
    levels = n // 2
    pair = me + 1 - 2 * half
    quarter = 2 * chunk

    def send(src, dst, out_sem, in_sem, peer):
        copy = pltpu.make_async_remote_copy(
            src_ref=src, dst_ref=dst, send_sem=out_sem, recv_sem=in_sem,
            device_id={"space": peer}, device_id_type=MESH,
        )
        copy.start()
        return copy

    def band(index, size):
        return pl.ds(pl.multiple_of(index * size, size), size)

    def pack(direction, real, imag):
        turned = jnp.where(row > col, -real, imag).T
        part[direction] = (jnp.where(row < col, real, imag) + turned).astype(jnp.bfloat16)

    def scatter(direction):
        copies = []
        for o in range(1, n):
            peer = lax.rem(me + o, n)
            copies.append(send(
                part.at[direction, band(peer, chunk)], landed.at[o],
                rs_send.at[direction, o], rs_recv.at[direction, o], peer,
            ))
        return copies

    def gather(direction, copies):
        total = part[direction, band(me, chunk)].astype(jnp.float32)
        for o in range(1, n):
            copies[o - 1].wait_recv()
            total = total + landed[o].astype(jnp.float32)
        low[direction] = total.astype(jnp.bfloat16)
        gathered[direction, band(me, chunk)] = low[direction]
        return [
            send(
                low.at[direction], gathered.at[direction, band(me, chunk)],
                ag_send.at[direction, o], ag_recv.at[direction, o], lax.rem(me + o, n),
            )
            for o in range(1, n)
        ]

    def level_peer(o):
        to = lax.rem(level + o, levels)
        return to, to * 2 + half

    def scatter_levels(direction):
        copies = []
        for o in range(1, levels):
            to, peer = level_peer(o)
            copies.append(send(
                part.at[direction, band(to, quarter)], landed_levels.at[direction, o],
                rs_send.at[direction, o], rs_recv.at[direction, o], peer,
            ))
        return copies

    def scatter_pair(direction, copies):
        total = part[direction, band(level, quarter)].astype(jnp.float32)
        for o in range(1, levels):
            copies[o - 1].wait_recv()
            total = total + landed_levels[direction, o].astype(jnp.float32)
        quarters[direction] = total.astype(jnp.bfloat16)
        return send(
            quarters.at[direction, band(1 - half, chunk)], landed_pair.at[direction],
            rs_send.at[direction, 0], rs_recv.at[direction, 0], pair,
        )

    def gather_levels(direction, copy):
        copy.wait_recv()
        total = quarters[direction, band(half, chunk)].astype(jnp.float32)
        low[direction] = (total + landed_pair[direction].astype(jnp.float32)).astype(jnp.bfloat16)
        gathered[direction, band(me, chunk)] = low[direction]
        copies = [send(
            low.at[direction], gathered.at[direction, band(me, chunk)],
            ag_send.at[direction, 0], ag_recv.at[direction, 0], pair,
        )]
        for o in range(1, levels):
            copies.append(send(
                low.at[direction], gathered.at[direction, band(me, chunk)],
                ag_send.at[direction, o], ag_recv.at[direction, o], level_peer(o)[1],
            ))
        return copies

    def gather_pair(direction, copies):
        passed = []
        for o in range(1, levels):
            copies[o].wait_recv()
            rows = band(lax.rem(level - o + levels, levels) * 2 + half, chunk)
            passed.append(send(
                gathered.at[direction, rows], gathered.at[direction, rows],
                ag_send.at[direction, levels + o], ag_recv.at[direction, levels + o], pair,
            ))
        return copies[:1] + passed

    def keep(direction, sends):
        for copy in sends:
            copy.wait_recv()
        packed = gathered[direction].astype(jnp.float32)
        flipped = packed.T
        upper = row < col
        minus_real = jnp.where(upper, -packed, jnp.where(row > col, flipped, 0.0)).astype(jnp.bfloat16)
        imag = jnp.where(upper, flipped, packed)
        elem_ref[direction, 0:K, 0:K] = minus_real
        elem_ref[direction, K : 2 * K, K : 2 * K] = minus_real
        elem_ref[direction, 0:K, K : 2 * K] = imag.astype(jnp.bfloat16)
        elem_ref[direction, K : 2 * K, 0:K] = (-imag).astype(jnp.bfloat16)

    own = lambda ri, c: v_ref[ri, c]
    first = {}
    for direction, which in ((0, 0), (2, 1)):
        for ri in range(2):
            for c in range(3):
                shifted[ri, c] = jnp.dot(
                    tables[which], v_ref[ri, c], preferred_element_type=jnp.float32
                ).astype(jnp.bfloat16)
        mix(link_ref, direction, False, 0, sites, lambda ri, c, rows: shifted[ri, c, rows], mixed)
        pack(direction, *overlap(own, lambda ri, c: mixed[ri, c]))
        first[direction] = scatter_levels(direction)

    swap.wait()
    order = spin_order(True)
    columns = swapped.shape[1]
    for ri in range(2):
        for b in range(SPIN):
            sorted_block = jnp.dot(
                swapped[ri, :, b * K : (b + 1) * K], order, preferred_element_type=jnp.float32
            ).astype(jnp.bfloat16)
            for spin in range(SPIN):
                at = ri * K + b * (K // SPIN)
                spread_ref[spin * columns : (spin + 1) * columns, at : at + K // SPIN] = sorted_block[
                    :, spin * (K // SPIN) : (spin + 1) * (K // SPIN)
                ]
    second = {direction: scatter_pair(direction, first[direction]) for direction in (0, 2)}

    down.wait_recv()
    mix(link_ref, 1, False, 0, split, lambda ri, c, rows: down_in[ri, c, rows], mixed_lo)
    real, imag = overlap(lambda ri, c: v_ref[ri, c, 0:split], lambda ri, c: mixed_lo[ri, c])
    third = {direction: gather_levels(direction, second[direction]) for direction in (0, 2)}
    up.wait_recv()
    real_up, imag_up = overlap(lambda ri, c: up_in[ri, c], lambda ri, c: v_ref[ri, c, split:sites])
    pack(1, real + real_up, imag + imag_up)
    scattered = scatter(1)
    last = {direction: gather_pair(direction, third[direction]) for direction in (0, 2)}
    sent = gather(1, scattered)
    for direction in (0, 2):
        keep(direction, last[direction])
    keep(1, sent)
    down.wait_send()
    up.wait_send()
    for copy in scattered + sent:
        copy.wait_send()
    for direction in (0, 2):
        for copy in first[direction] + [second[direction]] + third[direction] + last[direction][1:]:
            copy.wait_send()


def spin_order(apart):
    near = lax.broadcasted_iota(jnp.int32, (K, K), 0 if apart else 1)
    far = lax.broadcasted_iota(jnp.int32, (K, K), 1 if apart else 0)
    part = K // SPIN
    spin = near & (SPIN - 1)
    hit = far * SPIN == spin * (part * SPIN - 1) + near
    return jnp.where(hit, 1.0, 0.0).astype(jnp.bfloat16)


def upper_rows(sites):
    return (sites + 31) // 32 * 16


def finish_kernel(dirs_ref, elem_ref, spread_ref, out_ref):
    columns = out_ref.shape[2]
    part = K // SPIN
    back = spin_order(False)
    result = jnp.dot(
        spread_ref[...], elem_ref[dirs_ref[pl.program_id(0)]], preferred_element_type=jnp.float32
    ).astype(jnp.bfloat16)
    stacked = jnp.concatenate(
        [
            jnp.concatenate(
                [
                    result[s * columns : (s + 1) * columns, ri * K + b * part : ri * K + (b + 1) * part]
                    for s in range(SPIN)
                ],
                axis=1,
            )
            for ri in range(2)
            for b in range(SPIN)
        ],
        axis=0,
    )
    mixed = jnp.dot(stacked, back, preferred_element_type=jnp.float32).astype(jnp.bfloat16)
    for ri in range(2):
        for b in range(SPIN):
            at = (ri * SPIN + b) * columns
            out_ref[0, ri, :, b * K : (b + 1) * K] = mixed[at : at + columns]


def finish_packed(dirs, elem, spread, columns):
    return pl.pallas_call(
        finish_kernel,
        grid=(3,),
        out_shape=jax.ShapeDtypeStruct((3, 2, columns, K * SPIN), jnp.bfloat16),
        in_specs=[
            pl.BlockSpec(memory_space=pltpu.SMEM),
            pl.BlockSpec(memory_space=pltpu.VMEM),
            pl.BlockSpec(memory_space=pltpu.VMEM),
        ],
        out_specs=pl.BlockSpec((1, 2, columns, K * SPIN), lambda j: (j, 0, 0, 0)),
        compiler_params=pltpu.CompilerParams(vmem_limit_bytes=40 * 2**20),
    )(dirs, elem, spread)


def shift_tables(tables, sites):
    here = lax.broadcasted_iota(jnp.int32, (sites, sites), 0)
    there = lax.broadcasted_iota(jnp.int32, (sites, sites), 1)
    step = there - here
    tables[0] = jnp.where((step == LZ) | (step == LZ - sites), 1.0, 0.0).astype(jnp.bfloat16)
    first = there == 0
    for x in range(1, LX):
        first = first | (there == x * LZ)
    wanted = jnp.where(first, 1 - LZ, 1)
    tables[1] = jnp.where(step == wanted, 1.0, 0.0).astype(jnp.bfloat16)


def exchange(eigvecs, links, peram):
    n = lax.axis_size("space")
    sites = LX * LZ
    split = upper_rows(sites)
    columns = peram.shape[2]
    bf, chunk = jnp.bfloat16, K // n
    vmem = pl.BlockSpec(memory_space=pltpu.VMEM)
    hbm = pl.BlockSpec(memory_space=pltpu.HBM)
    return pl.pallas_call(
        functools.partial(halo_kernel, n),
        out_shape=(
            jax.ShapeDtypeStruct((3, 2 * K, 2 * K), bf),
            jax.ShapeDtypeStruct((SPIN * columns, 2 * K), bf),
        ),
        in_specs=[hbm, vmem, hbm],
        out_specs=(vmem, vmem),
        scratch_shapes=[
            pltpu.VMEM((2, 3, sites, K), bf),
            pltpu.VMEM((2, sites, sites), bf),
            pltpu.VMEM((2, 3, sites, K), bf),
            pltpu.VMEM((2, 3, sites, K), bf),
            pltpu.VMEM((2, 3, split, K), bf),
            pltpu.VMEM((2, 3, sites - split, K), bf),
            pltpu.VMEM((2, 3, sites - split, K), bf),
            pltpu.VMEM((2, 3, split, K), bf),
            pltpu.VMEM((3, K, K), bf),
            pltpu.VMEM((3, K, K), bf),
            pltpu.VMEM((3, chunk, K), bf),
            pltpu.VMEM((n, chunk, K), bf),
            pltpu.VMEM((3, n // 2, 2 * chunk, K), bf),
            pltpu.VMEM((3, chunk, K), bf),
            pltpu.VMEM((3, 2 * chunk, K), bf),
            pltpu.VMEM(peram.shape[1:], bf),
            pltpu.SemaphoreType.DMA,
            pltpu.SemaphoreType.DMA((3,)),
            pltpu.SemaphoreType.DMA((3,)),
            pltpu.SemaphoreType.DMA((3, n)),
            pltpu.SemaphoreType.DMA((3, n)),
            pltpu.SemaphoreType.DMA((3, n)),
            pltpu.SemaphoreType.DMA((3, n)),
        ],
        compiler_params=pltpu.CompilerParams(
            collective_id=0, has_side_effects=True, vmem_limit_bytes=40 * 2**20
        ),
    )(
        jnp.transpose(eigvecs[0], (0, 2, 3, 1)),
        links[0].reshape(54, sites).T.astype(jnp.float32),
        peram[0],
    )


def on_device(eigvecs, links, dirs, peram):
    if halo_plan(eigvecs):
        elem, spread = exchange(eigvecs, links, peram)
        return finish_packed(dirs, elem, spread, peram.shape[2])[None]
    return general(eigvecs, links, dirs, peram)


def solution(mesh):
    placed = (
        P(("parts", "tm"), None, None, None, "space"),
        P(("parts", "tm"), None, None, None, None, "space"),
        P(),
        P(("parts", "tm"), None, "space", None),
    )
    return jax.shard_map(
        on_device,
        mesh=mesh,
        in_specs=placed,
        out_specs=P(("parts", "tm"), None, None, "space", None),
        check_vma=False,
    )
```
